512 devices in a mesh: row: 16 (over y, x_lo), col: 32 (over x_hi, z, core).
Axes of the slice: x: 4 (x_hi: 2, x_lo: 2; x = x_hi * 2 + x_lo), y: 8, z: 8, core: 2. Of those that a mesh axis runs over, the one named last changes fastest.
Arguments:
- tokens: bfloat16 [65536, 3584], P(('row', 'col')), may hold values from -6 to 6
- targets: bfloat16 [65536, 3584], P(('row', 'col')), may hold values from -6 to 6
- w_up: bfloat16 [32, 3584, 448], P('col', 'row'), may hold values from -6 to 6
- w_down: bfloat16 [16, 3584, 448], P('row', 'col'), may hold values from -6 to 6
- up_momentum: float32 [32, 3584, 448], P('col', 'row'), may hold values from -2 to 2
- down_momentum: float32 [16, 3584, 448], P('row', 'col'), may hold values from -2 to 2
- member_up: int32 [16, 32], replicated, may hold values from 0 to 1, as said below
- member_down: int32 [16, 32], replicated, may hold values from 0 to 1, as said below
- path_rate: float32 [16, 32], replicated, may hold values from 0.1 to 1
Outputs:
- new_up: bfloat16 [32, 3584, 448], P('col', 'row')
- new_up_momentum: float32 [32, 3584, 448], P('col', 'row')
- new_down: bfloat16 [16, 3584, 448], P('row', 'col')
- new_down_momentum: float32 [16, 3584, 448], P('row', 'col')
The draws below stay inside these ranges and needn't reach their ends.
Inputs may be any that keep to these rules, and one draw needn't show every extreme that they name: Every column of member_up holds at least one 1. Every row of member_down holds at least one 1.
All inputs are finite; a program needn't handle non-finite values. Where the reference program divides by a largest or mean magnitude, that divisor is 1e-20 or more.
Results may differ from the reference program's by a relative error of at most 0.006.
Values may be sent and summed in bfloat16 or wider, within the bound.
A program may use at most 64 MiB of HBM per device.

```python
import math
import jax
import jax.numpy as jnp
from jax import lax

D = 3584
H = 448
ROWS = 128
TOKENS = 65536
UP_MODULES = 32
DOWN_MODULES = 16
N_ROW = 16
N_COL = 32


def draw_member_up(key, part):
    first, second = jax.random.split(jax.random.fold_in(key, 11))
    flags = jax.random.randint(first, (N_ROW, N_COL), 0, 2).astype(jnp.int32)
    chosen = jax.random.randint(second, (1, N_COL), 0, N_ROW).astype(jnp.int32)
    places = lax.broadcasted_iota(jnp.int32, (N_ROW, N_COL), 0)
    return jnp.maximum(flags, (places == chosen).astype(jnp.int32))


def draw_member_down(key, part):
    first, second = jax.random.split(jax.random.fold_in(key, 23))
    flags = jax.random.randint(first, (N_ROW, N_COL), 0, 2).astype(jnp.int32)
    chosen = jax.random.randint(second, (N_ROW, 1), 0, N_COL).astype(jnp.int32)
    places = lax.broadcasted_iota(jnp.int32, (N_ROW, N_COL), 1)
    return jnp.maximum(flags, (places == chosen).astype(jnp.int32))


def shard_levels(own_key, dims, cuts, smallest, top_value):
    def one(dim, parts):
        draws = jax.random.uniform(jax.random.fold_in(jax.random.fold_in(own_key, 6), dim), (parts,), jnp.float32, smallest / len(cuts), top_value / len(cuts))
        return jnp.repeat(jnp.exp(draws), dims[dim] // parts).reshape((-1,) + (1,) * (len(dims) - dim - 1))

    level = one(*cuts[0])
    for cut in cuts[1:]:
        level = level * one(*cut)
    return level


def scatter_about(own_key, extent, deviation, reach, pieces=(), held_as=jnp.bfloat16):
    result = deviation * jax.random.normal(own_key, extent, jnp.float32)
    if pieces:
        result = result * shard_levels(own_key, extent, pieces, -0.22, 0.18)
    return jnp.clip(result, -reach, reach).astype(held_as)


def setup_inputs(seed: int = 0) -> dict:
    arg_keys = jax.random.split(jax.random.key(seed), 10)
    tokens = scatter_about(arg_keys[0], (TOKENS, D), 1.0, 6.0, ((0, 512),))
    targets = scatter_about(arg_keys[1], (TOKENS, D), 1.0, 6.0, ((0, 512),))
    w_up = scatter_about(arg_keys[2], (UP_MODULES, D, H), 1.0, 6.0, ((0, 32), (1, 16)))
    w_down = scatter_about(arg_keys[3], (DOWN_MODULES, D, H), 1.0, 6.0, ((0, 16), (1, 32)))
    up_momentum = scatter_about(arg_keys[4], (UP_MODULES, D, H), 0.3, 2.0, ((0, 32), (1, 16)), jnp.float32)
    down_momentum = scatter_about(arg_keys[5], (DOWN_MODULES, D, H), 0.3, 2.0, ((0, 16), (1, 32)), jnp.float32)
    member_up = draw_member_up(jax.random.fold_in(arg_keys[9], 71), 0)
    member_down = draw_member_down(jax.random.fold_in(arg_keys[9], 71), 0)
    path_rate = jnp.clip(jnp.exp(jax.random.uniform(arg_keys[8], (N_ROW, N_COL), jnp.float32, math.log(0.1), math.log(1.0))), 0.1, 1.0)
    return {"tokens": tokens, "targets": targets, "w_up": w_up, "w_down": w_down, "up_momentum": up_momentum, "down_momentum": down_momentum, "member_up": member_up, "member_down": member_down, "path_rate": path_rate}


def silu_slope(pre):
    sig = jax.nn.sigmoid(pre)
    return sig * (1.0 + pre * (1.0 - sig))

def forward(tokens_path, targets_path, up_matrix, down_matrix):
    pre = jnp.dot(tokens_path, up_matrix, preferred_element_type=jnp.float32) * D ** (-0.5)
    hidden_act = jax.nn.silu(pre).astype(jnp.bfloat16)
    mixed = lax.dot_general(hidden_act, down_matrix, (((1,), (1,)), ((), ())), preferred_element_type=jnp.float32) * H ** (-0.5)
    slope_out = (tokens_path.astype(jnp.float32) + mixed - targets_path.astype(jnp.float32)).astype(jnp.bfloat16)
    return (pre, hidden_act, slope_out)

def packed(grad, rate):
    spread = jnp.sqrt(lax.optimization_barrier(jnp.mean(grad * grad, axis=1, keepdims=True)) + 1e-05)
    unit = grad / (jnp.abs(grad) + spread)
    largest = lax.optimization_barrier(jnp.max(jnp.abs(unit), axis=1, keepdims=True)) + 1e-06
    return ((unit / largest).astype(jnp.bfloat16), rate * largest[:, 0])

def grad_up(tokens_path, targets_path, up_matrix, down_matrix):
    pre, hidden_act, slope_out = forward(tokens_path, targets_path, up_matrix, down_matrix)
    slope_hidden = jnp.dot(slope_out, down_matrix, preferred_element_type=jnp.float32) * H ** (-0.5)
    slope_pre = (slope_hidden * silu_slope(pre)).astype(jnp.bfloat16)
    return lax.dot_general(tokens_path, slope_pre, (((0,), (0,)), ((), ())), preferred_element_type=jnp.float32) * D ** (-0.5)

def grad_down(tokens_path, targets_path, up_matrix, down_matrix):
    pre, hidden_act, slope_out = forward(tokens_path, targets_path, up_matrix, down_matrix)
    return lax.dot_general(slope_out, hidden_act, (((0,), (0,)), ((), ())), preferred_element_type=jnp.float32) * H ** (-0.5)

def reference(tokens, targets, w_up, w_down, up_momentum, down_momentum, member_up, member_down, path_rate):
    token_grid = tokens.reshape(N_ROW, N_COL, ROWS, D)
    target_grid = targets.reshape(N_ROW, N_COL, ROWS, D)
    flags_up = member_up.astype(jnp.float32)
    flags_down = member_down.astype(jnp.float32)

    def phase_up(total, row_id):
        down_matrix = w_down[row_id]

        def one_path(tokens_path, targets_path, up_matrix, rate, flag):
            grad = grad_up(tokens_path, targets_path, up_matrix, down_matrix)
            quant, scales = packed(grad, rate)
            return flag * scales[:, None] * quant.astype(jnp.float32)
        terms = jax.vmap(one_path)(token_grid[row_id], target_grid[row_id], w_up, path_rate[row_id], flags_up[row_id])
        return (total + terms, None)
    start_up = jnp.zeros((N_COL, D, H), jnp.float32)
    total_up, unused = lax.scan(phase_up, start_up, jnp.arange(N_ROW, dtype=jnp.int32))
    average_up = total_up / lax.optimization_barrier(jnp.sum(flags_up, axis=0))[:, None, None]
    new_up_momentum = 0.9 * up_momentum + average_up
    new_up = (w_up.astype(jnp.float32) - 0.7 * (average_up + 0.9 * new_up_momentum)).astype(jnp.bfloat16)

    def phase_down(total, col_id):
        up_matrix = new_up[col_id]

        def one_path(tokens_path, targets_path, down_matrix, rate, flag):
            grad = grad_down(tokens_path, targets_path, up_matrix, down_matrix)
            quant, scales = packed(grad, rate)
            return flag * scales[:, None] * quant.astype(jnp.float32)
        terms = jax.vmap(one_path)(token_grid[:, col_id], target_grid[:, col_id], w_down, path_rate[:, col_id], flags_down[:, col_id])
        return (total + terms, None)
    start_down = jnp.zeros((N_ROW, D, H), jnp.float32)
    total_down, unused_down = lax.scan(phase_down, start_down, jnp.arange(N_COL, dtype=jnp.int32))
    average_down = total_down / lax.optimization_barrier(jnp.sum(flags_down, axis=1))[:, None, None]
    new_down_momentum = 0.9 * down_momentum + average_down
    new_down = (w_down.astype(jnp.float32) - 0.7 * (average_down + 0.9 * new_down_momentum)).astype(jnp.bfloat16)
    return (new_up, new_up_momentum, new_down, new_down_momentum)
```

```python
import jax
import jax.numpy as jnp
from jax import lax
from jax.experimental import pallas as pl
from jax.experimental.pallas import tpu as pltpu
from jax.sharding import Mesh
from jax.sharding import PartitionSpec as P

MESH = pl.DeviceIdType.MESH
F32 = jnp.float32
BF16 = jnp.bfloat16
AXES = {"y": 8, "xl": 2, "xh": 2, "z": 8, "core": 2}
ROW = ("y", "xl")
COL = ("xh", "z", "core")
N_ROW, N_COL = 16, 32
NT = (((1,), (1,)), ((), ()))


def shifted(axis, step):
    size = AXES[axis]
    return lax.rem(lax.axis_index(axis) + (step % size), size)


class Mail:
    def __init__(self, send_sems, recv_sems):
        self.send_sems, self.recv_sems = send_sems, recv_sems
        self.number = {}
        self.sent = []

    def copy(self, key, ref, device):
        number = self.number.setdefault(key, len(self.number))
        return pltpu.make_async_remote_copy(
            src_ref=ref[0],
            dst_ref=ref[1],
            send_sem=self.send_sems.at[number],
            recv_sem=self.recv_sems.at[number],
            device_id=device,
            device_id_type=MESH,
        )

    def send(self, key, src, dst, **steps):
        device = {axis: shifted(axis, step) for axis, step in steps.items()}
        copy = self.copy(key, (src, dst), device)
        copy.start()
        self.sent.append(copy)

    def wait(self, key, slot, axis):
        self.copy(key, (slot, slot), {axis: shifted(axis, 1)}).wait_recv()

    def finish(self):
        for copy in self.sent:
            copy.wait_send()


def gather_balanced(mail, name, slot, line, pair, arrived):
    def send(key, dl, dp, h, **steps):
        ref = slot(dl, dp, h)
        mail.send((name, *key, h), ref, ref, **steps)

    def wait(key, dl, dp, h, axis):
        mail.wait((name, *key, h), slot(dl, dp, h), axis)

    ways = (1, -1)
    for h in (0, 1):
        for way in ways:
            send(("l", way, 1, 0), 0, 0, h, **{line: way})
        send(("p", 0, 0), 0, 0, h, **{pair: 1})
    arrived(0, 0)
    yield
    for h in (0, 1):
        for way in ways:
            wait(("l", way, 1, 0), -way, 0, h, line)
            send(("l", way, 2, 0), -way, 0, h, **{line: way})
            send(("p", way, 1), -way, 0, h, **{pair: 1})
    for way in ways:
        arrived(-way, 0)
    yield
    for h in (0, 1):
        for way in ways:
            wait(("l", way, 2, 0), -2 * way, 0, h, line)
            send(("l", way, 3, 0), -2 * way, 0, h, **{line: way})
            send(("p", way, 2), -2 * way, 0, h, **{pair: 1})
    for h in (0, 1):
        wait(("p", 0, 0), 0, 1, h, pair)
    for way in ways:
        arrived(-2 * way, 0)
    arrived(0, 1)
    yield
    for h in (0, 1):
        for way in ways:
            wait(("l", way, 3, 0), -3 * way, 0, h, line)
            if way == 1 - 2 * h:
                send(("l", way, 4, 0), -3 * way, 0, h, **{line: way})
        for way in ways:
            wait(("p", way, 2), -2 * way, 1, h, pair)
            send(("l", way, 3, 1), -2 * way, 1, h, **{line: way})
    for h in (0, 1):
        for way in ways:
            wait(("p", way, 1), -way, 1, h, pair)
    for way in ways:
        arrived(-3 * way, 0)
        arrived(-2 * way, 1)
        arrived(-way, 1)
    yield
    for h in (0, 1):
        way = 1 - 2 * h
        wait(("l", way, 3, 1), -3 * way, 1, h, line)
        send(("l", way, 4, 1), -3 * way, 1, h, **{line: way})
    for h in (0, 1):
        way = 2 * h - 1
        wait(("l", way, 3, 1), -3 * way, 1, h, line)
    for way in ways:
        arrived(-3 * way, 1)
    for h in (0, 1):
        way = 1 - 2 * h
        wait(("l", way, 4, 0), -4 * way, 0, h, line)
    arrived(4, 0)
    for h in (0, 1):
        way = 1 - 2 * h
        wait(("l", way, 4, 1), -4 * way, 1, h, line)
    arrived(4, 1)
    yield


def gather_line(mail, name, slot, line, pair, arrived):
    def send(key, dl, dp, **steps):
        ref = slot(dl, dp)
        mail.send((name, *key), ref, ref, **steps)

    def wait(key, dl, dp, axis):
        mail.wait((name, *key), slot(dl, dp), axis)

    ways = (1, -1)
    send(("p",), 0, 0, **{pair: 1})
    for way in ways:
        send(("l", way, 1, 0), 0, 0, **{line: way})
    arrived(0, 0)
    yield
    wait(("p",), 0, 1, pair)
    for way in ways:
        send(("l", way, 1, 1), 0, 1, **{line: way})
    arrived(0, 1)
    for d in (1, 2, 3):
        yield
        for dp in (0, 1):
            for way in ways:
                wait(("l", way, d, dp), -d * way, dp, line)
                if d < 3 or way == 1 - 2 * dp:
                    send(("l", way, d + 1, dp), -d * way, dp, **{line: way})
                arrived(-d * way, dp)
    yield
    for dp in (0, 1):
        wait(("l", 1 - 2 * dp, 4, dp), 4, dp, line)
        arrived(4, dp)
    yield


def packed_sum(grad, weight):
    size = jnp.abs(grad)
    spread = jnp.sqrt(jnp.mean(grad * grad, axis=-1, keepdims=True) + 1e-05)
    top = jnp.max(size, axis=-1, keepdims=True)
    largest = top / (top + spread) + 1e-06
    quant = (grad / ((size + spread) * largest)).astype(BF16)
    return quant.astype(F32) * (weight * largest)


def kernel(
    x_ref,
    t_ref,
    wu_ref,
    wd_ref,
    mu_ref,
    md_ref,
    member_up,
    member_down,
    path_rate,
    new_up,
    new_mu,
    new_down,
    new_md,
    up_all,
    down_all,
    fresh_all,
    x_out,
    x_in,
    d_out,
    d_in,
    dpre_all,
    hid_all,
    dh_ref,
    acc_up,
    acc_down,
    send_sems,
    recv_sems,
    local_sems,
):
    rows, width = x_ref.shape
    hidden = wu_ref.shape[1]
    inv_width = width ** (-0.5)
    inv_hidden = hidden ** (-0.5)
    own_up, own_down = wu_ref.shape[0], wd_ref.shape[0]
    step = 512
    steps = width // step
    y, xl = lax.axis_index("y"), lax.axis_index("xl")
    xh, z, core = lax.axis_index("xh"), lax.axis_index("z"), lax.axis_index("core")
    row = y * 2 + xl
    col = xh * 16 + z * 2 + core

    row_peers = [
        (dl, dp) for dl in (4, 3, -3, 2, -2, 1, -1, 0) for dp in (1, 0) if (dl, dp) != (0, 0)
    ]
    col_peers = [
        (dl, dp, dc)
        for dl in (4, 3, -3, 2, -2, 1, -1, 0)
        for dp in (1, 0)
        for dc in (1, 0)
        if (dl, dp, dc) != (0, 0, 0)
    ]

    barrier = pltpu.get_barrier_semaphore()
    for dl, dp in row_peers:
        pl.semaphore_signal(
            barrier,
            inc=1,
            device_id={"y": shifted("y", dl), "xl": shifted("xl", dp)},
            device_id_type=MESH,
        )
    for dl, dp, dc in col_peers:
        pl.semaphore_signal(
            barrier,
            inc=1,
            device_id={
                "z": shifted("z", dl),
                "xh": shifted("xh", dp),
                "core": shifted("core", dc),
            },
            device_id_type=MESH,
        )

    def row_of(dl, dp):
        return shifted("y", dl) * 2 + shifted("xl", dp)

    def col_of(dl, dp, dc):
        return shifted("xh", dp) * 16 + shifted("z", dl) * 2 + shifted("core", dc)

    def cut(ref, number, size, start=0, length=None):
        length = size if length is None else length
        return ref.at[pl.ds(pl.multiple_of(number * size + start, 16), length)]

    def nothing(dl, dp):
        pass

    mail = Mail(send_sems, recv_sems)
    half_up, half_hid = own_up // 2, hidden // 2

    own_copies = [
        pltpu.make_async_copy(wu_ref, cut(up_all, row, own_up), local_sems.at[0]),
        pltpu.make_async_copy(wd_ref, cut(down_all, col, own_down), local_sems.at[1]),
    ]
    for copy in own_copies:
        copy.start()
    for copy in own_copies:
        copy.wait()

    pl.semaphore_wait(barrier, len(row_peers) + len(col_peers))

    def up_slot(dl, dp, h):
        return cut(up_all, row_of(dl, dp), own_up, h * half_up, half_up)

    def fresh_slot(dl, dp, h):
        return cut(fresh_all, row_of(dl, dp), own_up, h * half_up, half_up)

    def down_slot(dl, dp, dc=0):
        return cut(down_all, col_of(dl, dp, dc), own_down)

    def dpre_slot(dl, dp, h):
        return dpre_all.at[row_of(dl, dp), pl.ds(h * half_hid, half_hid)]

    def hid_slot(dl, dp, h):
        return hid_all.at[col_of(dl, dp, 0), pl.ds(h * half_hid, half_hid)]

    def hid_whole(dl, dp, dc):
        return hid_all.at[col_of(dl, dp, dc)]

    def down_arrived(dl, dp):
        ref = down_slot(dl, dp)
        mail.send(("down sibling", dl % 8, dp), ref, ref, core=1)

    def hid_arrived(dl, dp):
        ref = hid_whole(dl, dp, 0)
        mail.send(("hid sibling", dl % 8, dp), ref, ref, core=1)

    pairs = [(dl, dp) for dl in range(8) for dp in range(2)]

    up_steps = gather_balanced(mail, "up", up_slot, "y", "xl", nothing)
    down_steps = gather_line(mail, "down", down_slot, "z", "xh", down_arrived)
    next(up_steps)
    next(down_steps)

    def turn(j, carry):
        at = pl.multiple_of(j * 128, 128)
        tile = x_ref[:, pl.ds(at, 128)].astype(F32)
        x_out[pl.ds(at, 128), :] = tile.T.astype(BF16)
        other = t_ref[:, pl.ds(at, 128)].astype(F32)
        d_out[pl.ds(at, 128), :] = (tile - other).T.astype(BF16)
        return carry

    lax.fori_loop(0, width // 128, turn, 0)
    next(up_steps)
    next(down_steps)
    next(up_steps)
    next(down_steps)
    next(up_steps)
    for dl, dp in row_peers:
        mail.send(
            ("tokens", dl % 8, dp),
            cut(x_out, row_of(dl, dp), own_up),
            cut(x_in, row, own_up),
            y=dl,
            xl=dp,
        )
    next(down_steps)
    next(up_steps)
    next(down_steps)
    for dl, dp, dc in col_peers:
        mail.send(
            ("delta", dl % 8, dp, dc),
            cut(d_out, col_of(dl, dp, dc), own_down),
            cut(d_in, col, own_down),
            z=dl,
            xh=dp,
            core=dc,
        )
    next(down_steps)
    x_in[pl.ds(pl.multiple_of(row * own_up, 16), own_up), :] = x_out[
        pl.ds(pl.multiple_of(row * own_up, 16), own_up), :
    ]
    d_in[pl.ds(pl.multiple_of(col * own_down, 16), own_down), :] = d_out[
        pl.ds(pl.multiple_of(col * own_down, 16), own_down), :
    ]

    def project(weights):
        def body(k, total):
            at = pl.multiple_of(k * step, step)
            return total + jnp.dot(
                x_ref[:, pl.ds(at, step)],
                weights[pl.ds(at, step), :],
                preferred_element_type=F32,
            )

        return lax.fori_loop(0, steps, body, jnp.zeros((rows, hidden), F32)) * inv_width

    pre = project(up_all)
    sig = jax.nn.sigmoid(pre)
    hid = (pre * sig).astype(BF16)
    slope = sig * (1.0 + pre * (1.0 - sig))
    for dl, dp in pairs:
        mail.wait(("down sibling", dl, dp), down_slot(dl, dp, 1), "core")

    dh_ref[...] = jnp.zeros_like(dh_ref)

    def back(k, carry):
        at = pl.multiple_of(k * step, step)
        part = down_all[pl.ds(at, step), :]
        mixed = lax.dot_general(hid, part, NT, preferred_element_type=F32) * inv_hidden
        dy = (
            x_ref[:, pl.ds(at, step)].astype(F32) + mixed - t_ref[:, pl.ds(at, step)].astype(F32)
        ).astype(BF16)
        dh_ref[...] += jnp.dot(dy, part, preferred_element_type=F32)
        return carry

    lax.fori_loop(0, steps, back, 0)
    dpre = dh_ref[...] * inv_hidden * slope
    dpre_all[row] = dpre.T.astype(BF16)

    for _ in gather_balanced(mail, "dpre", dpre_slot, "y", "xl", nothing):
        pass
    for dl, dp in row_peers:
        mail.wait(("tokens", dl % 8, dp), cut(x_in, row_of(-dl, dp), own_up), "y")

    acc_up[...] = jnp.zeros_like(acc_up)

    def up_path(p, count):
        at = pl.multiple_of(p * own_up, 16)
        grad = (
            lax.dot_general(
                x_in[pl.ds(at, own_up), :], dpre_all[p], NT, preferred_element_type=F32
            )
            * inv_width
        )
        flag = member_up[p, col].astype(F32)
        acc_up[...] += packed_sum(grad, flag * path_rate[p, col])
        return count + flag

    count_up = lax.fori_loop(0, N_ROW, up_path, jnp.float32(0.0))
    average = acc_up[...] / count_up
    momentum = 0.9 * mu_ref[...] + average
    new_mu[...] = momentum
    fresh = (wu_ref[...].astype(F32) - 0.7 * (average + 0.9 * momentum)).astype(BF16)
    new_up[...] = fresh
    fresh_all[pl.ds(pl.multiple_of(row * own_up, 16), own_up), :] = fresh

    for _ in gather_balanced(mail, "fresh", fresh_slot, "y", "xl", nothing):
        pass
    pre_again = project(fresh_all)
    hid_again = pre_again * jax.nn.sigmoid(pre_again)
    hid_all[col] = hid_again.T.astype(BF16)

    for _ in gather_balanced(mail, "hid", hid_slot, "z", "xh", hid_arrived):
        pass
    for dl, dp, dc in col_peers:
        mail.wait(("delta", dl % 8, dp, dc), cut(d_in, col_of(-dl, dp, dc), own_down), "z")
    for dl, dp in pairs:
        mail.wait(("hid sibling", dl, dp), hid_whole(dl, dp, 1), "core")

    acc_down[...] = jnp.zeros_like(acc_down)

    def down_path(q, count):
        at = pl.multiple_of(q * own_down, 16)
        acts = hid_all[q]
        mixed = jnp.dot(wd_ref[...], acts, preferred_element_type=F32) * inv_hidden
        dy = (d_in[pl.ds(at, own_down), :].astype(F32) + mixed).astype(BF16)
        grad = lax.dot_general(dy, acts, NT, preferred_element_type=F32) * inv_hidden
        flag = member_down[row, q].astype(F32)
        acc_down[...] += packed_sum(grad, flag * path_rate[row, q])
        return count + flag

    count_down = lax.fori_loop(0, N_COL, down_path, jnp.float32(0.0))
    average_down = acc_down[...] / count_down
    momentum_down = 0.9 * md_ref[...] + average_down
    new_md[...] = momentum_down
    new_down[...] = (
        wd_ref[...].astype(F32) - 0.7 * (average_down + 0.9 * momentum_down)
    ).astype(BF16)
    mail.finish()


def per_device(
    tokens, targets, w_up, w_down, up_momentum, down_momentum, member_up, member_down, path_rate
):
    rows, width = tokens.shape
    own_up, hidden = w_up.shape[1:]
    own_down = w_down.shape[1]
    vmem = pl.BlockSpec(memory_space=pltpu.VMEM)
    smem = pl.BlockSpec(memory_space=pltpu.SMEM)
    messages = 256
    outs = pl.pallas_call(
        kernel,
        out_shape=(
            jax.ShapeDtypeStruct((own_up, hidden), BF16),
            jax.ShapeDtypeStruct((own_up, hidden), F32),
            jax.ShapeDtypeStruct((own_down, hidden), BF16),
            jax.ShapeDtypeStruct((own_down, hidden), F32),
        ),
        in_specs=[vmem] * 6 + [smem] * 3,
        out_specs=(vmem,) * 4,
        scratch_shapes=[
            pltpu.VMEM((width, hidden), BF16),
            pltpu.VMEM((width, hidden), BF16),
            pltpu.VMEM((width, hidden), BF16),
            pltpu.VMEM((width, rows), BF16),
            pltpu.VMEM((width, rows), BF16),
            pltpu.VMEM((width, rows), BF16),
            pltpu.VMEM((width, rows), BF16),
            pltpu.VMEM((N_ROW, hidden, rows), BF16),
            pltpu.VMEM((N_COL, hidden, rows), BF16),
            pltpu.VMEM((rows, hidden), F32),
            pltpu.VMEM((own_up, hidden), F32),
            pltpu.VMEM((own_down, hidden), F32),
            pltpu.SemaphoreType.DMA((messages,)),
            pltpu.SemaphoreType.DMA((messages,)),
            pltpu.SemaphoreType.DMA((2,)),
        ],
        compiler_params=pltpu.CompilerParams(
            collective_id=0, has_side_effects=True, vmem_limit_bytes=56 * 1024 * 1024
        ),
        name="path_mixture",
    )(
        tokens,
        targets,
        w_up[0],
        w_down[0],
        up_momentum[0],
        down_momentum[0],
        member_up,
        member_down,
        path_rate,
    )
    return tuple(out[None] for out in outs)


def solution(mesh):
    torus = Mesh(mesh.devices.reshape(tuple(AXES.values())), tuple(AXES))
    placed = (
        P(ROW + COL, None),
        P(ROW + COL, None),
        P(COL, ROW, None),
        P(ROW, COL, None),
        P(COL, ROW, None),
        P(ROW, COL, None),
        P(),
        P(),
        P(),
    )
    return jax.shard_map(
        per_device,
        mesh=torus,
        in_specs=placed,
        out_specs=(
            P(COL, ROW, None),
            P(COL, ROW, None),
            P(ROW, COL, None),
            P(ROW, COL, None),
        ),
        check_vma=False,
    )
```

```python
import functools

import jax
import jax.numpy as jnp
from jax import lax
from jax.experimental import pallas as pl
from jax.experimental.pallas import tpu as pltpu
from jax.sharding import Mesh
from jax.sharding import PartitionSpec as P

MESH = pl.DeviceIdType.MESH
F32 = jnp.float32
BF16 = jnp.bfloat16
AXES = {"y": 8, "xl": 2, "xh": 2, "z": 8, "core": 2}
ROW = ("y", "xl")
COL = ("xh", "z", "core")
N_ROW, N_COL = 16, 32
NT = (((1,), (1,)), ((), ()))


def shifted(axis, step):
    size = AXES[axis]
    return lax.rem(lax.axis_index(axis) + (step % size), size)


class Mail:
    def __init__(self, send_sems, recv_sems):
        self.send_sems, self.recv_sems = send_sems, recv_sems
        self.number = {}
        self.sent = []

    def copy(self, key, ref, device):
        number = self.number.setdefault(key, len(self.number))
        return pltpu.make_async_remote_copy(
            src_ref=ref[0],
            dst_ref=ref[1],
            send_sem=self.send_sems.at[number],
            recv_sem=self.recv_sems.at[number],
            device_id=device,
            device_id_type=MESH,
        )

    def send(self, key, src, dst, **steps):
        device = {axis: shifted(axis, step) for axis, step in steps.items()}
        copy = self.copy(key, (src, dst), device)
        copy.start()
        self.sent.append(copy)

    def wait(self, key, slot, axis):
        self.copy(key, (slot, slot), {axis: shifted(axis, 1)}).wait_recv()

    def finish(self):
        for copy in self.sent:
            copy.wait_send()


def gather_balanced(mail, name, slot, line, pair):
    def send(key, dl, dp, h, **steps):
        ref = slot(dl, dp, h)
        mail.send((name, *key, h), ref, ref, **steps)

    def wait(key, dl, dp, h, axis):
        mail.wait((name, *key, h), slot(dl, dp, h), axis)

    ways = (1, -1)
    for h in (0, 1):
        for way in ways:
            send(("l", way, 1, 0), 0, 0, h, **{line: way})
        send(("p", 0, 0), 0, 0, h, **{pair: 1})
    yield
    for h in (0, 1):
        for way in ways:
            wait(("l", way, 1, 0), -way, 0, h, line)
            send(("l", way, 2, 0), -way, 0, h, **{line: way})
            send(("p", way, 1), -way, 0, h, **{pair: 1})
    yield
    for h in (0, 1):
        for way in ways:
            wait(("l", way, 2, 0), -2 * way, 0, h, line)
            send(("l", way, 3, 0), -2 * way, 0, h, **{line: way})
            send(("p", way, 2), -2 * way, 0, h, **{pair: 1})
    for h in (0, 1):
        wait(("p", 0, 0), 0, 1, h, pair)
    yield
    for h in (0, 1):
        for way in ways:
            wait(("l", way, 3, 0), -3 * way, 0, h, line)
            if way == 1 - 2 * h:
                send(("l", way, 4, 0), -3 * way, 0, h, **{line: way})
        for way in ways:
            wait(("p", way, 2), -2 * way, 1, h, pair)
            send(("l", way, 3, 1), -2 * way, 1, h, **{line: way})
    for h in (0, 1):
        for way in ways:
            wait(("p", way, 1), -way, 1, h, pair)
    yield
    for h in (0, 1):
        way = 1 - 2 * h
        wait(("l", way, 3, 1), -3 * way, 1, h, line)
        send(("l", way, 4, 1), -3 * way, 1, h, **{line: way})
    yield
    for h in (0, 1):
        way = 2 * h - 1
        wait(("l", way, 3, 1), -3 * way, 1, h, line)
    for dp in (0, 1):
        for h in (0, 1):
            way = 1 - 2 * h
            wait(("l", way, 4, dp), -4 * way, dp, h, line)
    yield


ORDER = (
    (0, 0),
    (-1, 0),
    (1, 0),
    (-2, 0),
    (2, 0),
    (0, 1),
    (-3, 0),
    (3, 0),
    (-2, 1),
    (2, 1),
    (-1, 1),
    (1, 1),
    (-3, 1),
    (3, 1),
    (4, 0),
    (4, 1),
)
READY = (None, (0, 3), (3, 6), (6, 9), (9, 12), (12, 16))


def picked(place, first, last, values):
    found = jnp.int32(values[first])
    for number in range(first + 1, last):
        found = jnp.where(place == number, jnp.int32(values[number]), found)
    return found


def scatter_balanced(mail, name, part, outgoing, incoming, kept, line, pair, result):
    places = {}

    def place(key):
        return places.setdefault(key, len(places))

    def send(key, value, **steps):
        at = place(key)
        outgoing[at] = value.astype(BF16)
        mail.send((name, *key), outgoing.at[at], incoming.at[at], **steps)

    def take(key, axis):
        at = place(key)
        mail.wait((name, *key), incoming.at[at], axis)
        return incoming[at].astype(F32)

    ways = (1, -1)
    for dp in (0, 1):
        for h in (0, 1):
            way = 1 - 2 * h
            send(("l", way, 4, dp, h), part(4, dp, h), **{line: way})
    yield
    for h in (0, 1):
        way = 2 * h - 1
        for dp in (0, 1):
            send(("l", way, 3, dp, h), part(3 * way, dp, h), **{line: way})
    for h in (0, 1):
        way = 1 - 2 * h
        for dp in (1, 0):
            total = part(3 * way, dp, h) + take(("l", way, 4, dp, h), line)
            send(("l", way, 3, dp, h), total, **{line: way})
    yield
    for h in (0, 1):
        for way in (2 * h - 1, 1 - 2 * h):
            total = part(2 * way, 1, h) + take(("l", way, 3, 1, h), line)
            send(("p", way, 2, h), total, **{pair: 1})
    for h in (0, 1):
        for way in (2 * h - 1, 1 - 2 * h):
            total = part(2 * way, 0, h) + take(("l", way, 3, 0, h), line)
            kept[2 * h + ways.index(way)] = total
    for h in (0, 1):
        for way in ways:
            send(("p", way, 1, h), part(way, 1, h), **{pair: 1})
    yield
    for h in (0, 1):
        for way in (2 * h - 1, 1 - 2 * h):
            total = kept[2 * h + ways.index(way)] + take(("p", way, 2, h), pair)
            send(("l", way, 2, h), total, **{line: way})
    for h in (0, 1):
        send(("p", 0, 0, h), part(0, 1, h), **{pair: 1})
    yield
    for h in (0, 1):
        for way in ways:
            total = part(way, 0, h) + take(("p", way, 1, h), pair)
            total = total + take(("l", way, 2, h), line)
            send(("l", way, 1, h), total, **{line: way})
    yield
    half = result.shape[0] // 2
    for h in (0, 1):
        total = part(0, 0, h) + take(("p", 0, 0, h), pair)
        for way in ways:
            total = total + take(("l", way, 1, h), line)
        result[pl.ds(h * half, half), :] = total
    yield


def gather_line(mail, name, slot, line, pair, arrived):
    def send(key, dl, dp, **steps):
        ref = slot(dl, dp)
        mail.send((name, *key), ref, ref, **steps)

    def wait(key, dl, dp, axis):
        mail.wait((name, *key), slot(dl, dp), axis)

    ways = (1, -1)
    send(("p",), 0, 0, **{pair: 1})
    for way in ways:
        send(("l", way, 1, 0), 0, 0, **{line: way})
    arrived(0, 0)
    yield
    wait(("p",), 0, 1, pair)
    for way in ways:
        send(("l", way, 1, 1), 0, 1, **{line: way})
    arrived(0, 1)
    for d in (1, 2, 3):
        yield
        for dp in (0, 1):
            for way in ways:
                wait(("l", way, d, dp), -d * way, dp, line)
                if d < 3 or way == 1 - 2 * dp:
                    send(("l", way, d + 1, dp), -d * way, dp, **{line: way})
                arrived(-d * way, dp)
    yield
    for dp in (0, 1):
        wait(("l", 1 - 2 * dp, 4, dp), 4, dp, line)
        arrived(4, dp)
    yield


def packed_sum(grad, weight):
    size = jnp.abs(grad)
    spread = jnp.sqrt(jnp.mean(grad * grad, axis=-1, keepdims=True) + 1e-05)
    top = jnp.max(size, axis=-1, keepdims=True)
    largest = top / (top + spread) + 1e-06
    quant = (grad / ((size + spread) * largest)).astype(BF16)
    return quant.astype(F32) * (weight * largest)


def kernel(
    x_hbm,
    t_hbm,
    wu_hbm,
    wd_hbm,
    mu_hbm,
    md_hbm,
    member_up,
    member_down,
    path_rate,
    new_up,
    new_mu,
    new_down,
    new_md,
    x_ref,
    t_ref,
    wu_ref,
    mu_ref,
    md_ref,
    turned,
    down_all,
    x_out,
    x_in,
    d_out,
    d_in,
    dpre_all,
    hid_all,
    dh_ref,
    pre_ref,
    kept,
    first_out,
    first_in,
    second_out,
    second_in,
    acc_up,
    acc_down,
    acc_sibling,
    send_sems,
    recv_sems,
    local_sems,
):
    rows, width = x_ref.shape
    own_up, hidden = wu_ref.shape
    own_down = md_ref.shape[0]
    inv_width = width ** (-0.5)
    inv_hidden = hidden ** (-0.5)
    step = 512
    steps = width // step
    y, xl = lax.axis_index("y"), lax.axis_index("xl")
    xh, z, core = lax.axis_index("xh"), lax.axis_index("z"), lax.axis_index("core")
    row = y * 2 + xl
    col = xh * 16 + z * 2 + core
    chip = xh * 8 + z

    peers = [(dl, dp) for dl in (4, 3, -3, 2, -2, 1, -1, 0) for dp in (1, 0) if dl or dp]
    barrier = pltpu.get_barrier_semaphore()
    for dl, dp in peers:
        for line, pair in (("y", "xl"), ("z", "xh")):
            pl.semaphore_signal(
                barrier,
                inc=1,
                device_id={line: shifted(line, dl), pair: shifted(pair, dp)},
                device_id_type=MESH,
            )
    pl.semaphore_signal(
        barrier, inc=1, device_id={"core": shifted("core", 1)}, device_id_type=MESH
    )

    def row_of(dl, dp):
        return lax.rem(y + (dl + 8), 8) * 2 + lax.rem(xl + dp, 2)

    def chip_of(dl, dp):
        return lax.rem(xh + dp, 2) * 8 + lax.rem(z + (dl + 8), 8)

    def col_of(dl, dp, dc):
        return chip_of(dl, dp) * 2 + lax.rem(core + dc, 2)

    def span(number, size):
        return pl.ds(pl.multiple_of(number * size, 16), size)

    def cut(ref, number, size):
        return ref.at[span(number, size)]

    mail = Mail(send_sems, recv_sems)
    half_hid = hidden // 2

    loads = [
        pltpu.make_async_copy(src, dst, local_sems.at[number])
        for number, (src, dst) in enumerate(
            (
                (x_hbm, x_ref),
                (wd_hbm, cut(down_all, col, own_down)),
                (wu_hbm, wu_ref),
                (t_hbm, t_ref),
                (mu_hbm, mu_ref),
                (md_hbm, md_ref),
            )
        )
    ]
    for load in loads:
        load.start()

    def down_slot(dl, dp, dc=0):
        return cut(down_all, col_of(dl, dp, dc), own_down)

    def dpre_slot(dl, dp, h):
        return dpre_all.at[row_of(dl, dp), pl.ds(h * half_hid, half_hid)]

    def hid_slot(dl, dp, h):
        return hid_all.at[chip_of(dl, dp), pl.ds(h * half_hid, half_hid)]

    def down_arrived(dl, dp):
        ref = down_slot(dl, dp)
        mail.send(("down sibling", dl % 8, dp), ref, ref, core=1)

    def send_delta(pairs):
        for dl, dp in peers:
            if dp in pairs:
                mail.send(
                    ("delta", dl % 8, dp),
                    cut(d_out, chip_of(dl, dp), 2 * own_down),
                    cut(d_in, chip, 2 * own_down),
                    z=dl,
                    xh=dp,
                )

    loads[0].wait()

    def turn(j, carry):
        at = pl.multiple_of(j * 128, 128)
        x_out[pl.ds(at, 128), :] = x_ref[:, pl.ds(at, 128)].astype(F32).T.astype(BF16)
        return carry

    lax.fori_loop(0, width // 128, turn, 0)
    loads[1].wait()
    pl.semaphore_wait(barrier, 2 * len(peers) + 1)
    for dl, dp in peers:
        mail.send(
            ("tokens", dl % 8, dp),
            cut(x_out, row_of(dl, dp), own_up),
            cut(x_in, row, own_up),
            y=dl,
            xl=dp,
        )
    down_steps = gather_line(mail, "down", down_slot, "z", "xh", down_arrived)
    next(down_steps)

    x_in[span(row, own_up), :] = x_out[span(row, own_up), :]
    loads[2].wait()
    turned[...] = wu_ref[...].astype(F32).T.astype(BF16)
    loads[3].wait()

    def turn_delta(j, carry):
        at = pl.multiple_of(j * 128, 128)
        other = t_ref[:, pl.ds(at, 128)].astype(F32)
        d_out[pl.ds(at, 128), :] = (x_ref[:, pl.ds(at, 128)].astype(F32) - other).T.astype(BF16)
        return carry

    lax.fori_loop(0, width // 128, turn_delta, 0)
    next(down_steps)

    here = {(0, 0)}

    def part(dl, dp, h):
        at = (dl % 8, dp)
        if at not in here:
            here.add(at)
            mail.wait(("tokens", -dl % 8, dp), cut(x_in, row_of(dl, dp), own_up), "y")
        return jnp.dot(
            turned[pl.ds(h * half_hid, half_hid), :],
            x_in[span(row_of(dl, dp), own_up), :],
            preferred_element_type=F32,
        )

    first = scatter_balanced(
        mail, "first", part, first_out, first_in, kept, "y", "xl", pre_ref
    )
    next(first)
    next(down_steps)
    next(first)
    next(down_steps)
    next(first)
    next(down_steps)
    next(first)
    next(down_steps)
    send_delta((0,))
    next(first)
    next(first)
    send_delta((1,))
    d_in[span(chip, 2 * own_down), :] = d_out[span(chip, 2 * own_down), :]

    pre = pre_ref[...].T * inv_width
    sig = jax.nn.sigmoid(pre)
    hid = (pre * sig).astype(BF16)
    slope = sig * (1.0 + pre * (1.0 - sig))
    for dl in range(8):
        for dp in range(2):
            mail.wait(("down sibling", dl, dp), down_slot(dl, dp, 1), "core")

    dh_ref[...] = jnp.zeros_like(dh_ref)

    def back(k, carry):
        at = pl.multiple_of(k * step, step)
        piece = down_all[pl.ds(at, step), :]
        mixed = lax.dot_general(hid, piece, NT, preferred_element_type=F32) * inv_hidden
        dy = (
            x_ref[:, pl.ds(at, step)].astype(F32) + mixed - t_ref[:, pl.ds(at, step)].astype(F32)
        ).astype(BF16)
        dh_ref[...] += jnp.dot(dy, piece, preferred_element_type=F32)
        return carry

    lax.fori_loop(0, steps, back, 0)
    dpre = dh_ref[...] * inv_hidden * slope
    dpre_all[row] = dpre.T.astype(BF16)

    def ordered(number, between):
        dl = picked(number, *between, [dl for dl, _ in ORDER])
        dp = picked(number, *between, [dp for _, dp in ORDER])
        return dl, dp

    acc_up[...] = jnp.zeros_like(acc_up)

    def up_path(between, number, carry):
        p = row_of(*ordered(number, between))
        grad = (
            lax.dot_general(
                x_in[span(p, own_up), :], dpre_all[p], NT, preferred_element_type=F32
            )
            * inv_width
        )
        acc_up[...] += packed_sum(grad, member_up[p, col].astype(F32) * path_rate[p, col])
        return carry

    for between, _ in zip(READY, gather_balanced(mail, "dpre", dpre_slot, "y", "xl")):
        if between:
            lax.fori_loop(*between, functools.partial(up_path, between), 0)
    count_up = lax.fori_loop(
        0, N_ROW, lambda p, count: count + member_up[p, col].astype(F32), jnp.float32(0.0)
    )
    loads[4].wait()
    loads[5].wait()
    average = acc_up[...] / count_up
    momentum = 0.9 * mu_ref[...] + average
    new_mu[...] = momentum
    fresh = wu_ref[...].astype(F32) - 0.7 * (average + 0.9 * momentum)
    new_up[...] = fresh.astype(BF16)
    turned[...] = fresh.T.astype(BF16)

    for _ in scatter_balanced(
        mail, "second", part, second_out, second_in, kept, "y", "xl", pre_ref
    ):
        pass
    pre_again = pre_ref[...] * inv_width
    hid_all[chip] = (pre_again * jax.nn.sigmoid(pre_again)).astype(BF16)

    acc_down[...] = jnp.zeros_like(acc_down)

    def down_path(between, number, carry):
        dl, dp = ordered(number, between)
        q = chip_of(dl, dp)
        acts = hid_all[q]
        mixed = (
            jnp.dot(
                down_all[span(chip, 2 * own_down), :], acts, preferred_element_type=F32
            )
            * inv_hidden
        )
        dy = (d_in[span(q, 2 * own_down), :].astype(F32) + mixed).astype(BF16)
        grad = lax.dot_general(dy, acts, NT, preferred_element_type=F32) * inv_hidden
        c = q * 2 + core
        acc_down[...] += packed_sum(grad, member_down[row, c].astype(F32) * path_rate[row, c])
        return carry

    for between, _ in zip(READY, gather_balanced(mail, "hid", hid_slot, "z", "xh")):
        if between:
            for dl, dp in ORDER[slice(*between)]:
                if dl or dp:
                    mail.wait(
                        ("delta", -dl % 8, dp), cut(d_in, chip_of(dl, dp), 2 * own_down), "z"
                    )
            lax.fori_loop(*between, functools.partial(down_path, between), 0)
    mail.send(("sums",), cut(acc_down, 1 - core, own_down), acc_sibling, core=1)
    count_down = lax.fori_loop(
        0, N_COL, lambda q, count: count + member_down[row, q].astype(F32), jnp.float32(0.0)
    )
    mail.wait(("sums",), acc_sibling, "core")
    average_down = (acc_down[span(core, own_down), :] + acc_sibling[...]) / count_down
    momentum_down = 0.9 * md_ref[...] + average_down
    new_md[...] = momentum_down
    own = down_all[span(col, own_down), :].astype(F32)
    new_down[...] = (own - 0.7 * (average_down + 0.9 * momentum_down)).astype(BF16)
    mail.finish()


def per_device(
    tokens, targets, w_up, w_down, up_momentum, down_momentum, member_up, member_down, path_rate
):
    rows, width = tokens.shape
    own_up, hidden = w_up.shape[1:]
    own_down = w_down.shape[1]
    vmem = pl.BlockSpec(memory_space=pltpu.VMEM)
    smem = pl.BlockSpec(memory_space=pltpu.SMEM)
    messages, sums = 200, 30
    outs = pl.pallas_call(
        kernel,
        out_shape=(
            jax.ShapeDtypeStruct((own_up, hidden), BF16),
            jax.ShapeDtypeStruct((own_up, hidden), F32),
            jax.ShapeDtypeStruct((own_down, hidden), BF16),
            jax.ShapeDtypeStruct((own_down, hidden), F32),
        ),
        in_specs=[pl.BlockSpec(memory_space=pl.ANY)] * 6 + [smem] * 3,
        out_specs=(vmem,) * 4,
        scratch_shapes=[
            pltpu.VMEM((rows, width), BF16),
            pltpu.VMEM((rows, width), BF16),
            pltpu.VMEM((own_up, hidden), BF16),
            pltpu.VMEM((own_up, hidden), F32),
            pltpu.VMEM((own_down, hidden), F32),
            pltpu.VMEM((hidden, own_up), BF16),
            pltpu.VMEM((width, hidden), BF16),
            pltpu.VMEM((width, rows), BF16),
            pltpu.VMEM((width, rows), BF16),
            pltpu.VMEM((width, rows), BF16),
            pltpu.VMEM((width, rows), BF16),
            pltpu.VMEM((N_ROW, hidden, rows), BF16),
            pltpu.VMEM((N_COL // 2, hidden, rows), BF16),
            pltpu.VMEM((rows, hidden), F32),
            pltpu.VMEM((hidden, rows), F32),
            pltpu.VMEM((4, hidden // 2, rows), F32),
            pltpu.VMEM((sums, hidden // 2, rows), BF16),
            pltpu.VMEM((sums, hidden // 2, rows), BF16),
            pltpu.VMEM((sums, hidden // 2, rows), BF16),
            pltpu.VMEM((sums, hidden // 2, rows), BF16),
            pltpu.VMEM((own_up, hidden), F32),
            pltpu.VMEM((2 * own_down, hidden), F32),
            pltpu.VMEM((own_down, hidden), F32),
            pltpu.SemaphoreType.DMA((messages,)),
            pltpu.SemaphoreType.DMA((messages,)),
            pltpu.SemaphoreType.DMA((6,)),
        ],
        compiler_params=pltpu.CompilerParams(
            collective_id=0, has_side_effects=True, vmem_limit_bytes=56 * 1024 * 1024
        ),
        name="path_mixture",
    )(
        tokens,
        targets,
        w_up[0],
        w_down[0],
        up_momentum[0],
        down_momentum[0],
        member_up,
        member_down,
        path_rate,
    )
    return tuple(out[None] for out in outs)


def solution(mesh):
    torus = Mesh(mesh.devices.reshape(tuple(AXES.values())), tuple(AXES))
    placed = (
        P(ROW + COL, None),
        P(ROW + COL, None),
        P(COL, ROW, None),
        P(ROW, COL, None),
        P(COL, ROW, None),
        P(ROW, COL, None),
        P(),
        P(),
        P(),
    )
    return jax.shard_map(
        per_device,
        mesh=torus,
        in_specs=placed,
        out_specs=(
            P(COL, ROW, None),
            P(COL, ROW, None),
            P(ROW, COL, None),
            P(ROW, COL, None),
        ),
        check_vma=False,
    )
```

```python
import functools

import jax
import jax.numpy as jnp
from jax import lax
from jax.experimental import pallas as pl
from jax.experimental.pallas import tpu as pltpu
from jax.sharding import Mesh
from jax.sharding import PartitionSpec as P

MESH = pl.DeviceIdType.MESH
F32 = jnp.float32
BF16 = jnp.bfloat16
AXES = {"y": 8, "xl": 2, "xh": 2, "z": 8, "core": 2}
ROW = ("y", "xl")
COL = ("xh", "z", "core")
N_ROW, N_COL = 16, 32
NT = (((1,), (1,)), ((), ()))


def shifted(axis, step):
    size = AXES[axis]
    return lax.rem(lax.axis_index(axis) + (step % size), size)


class Mail:
    def __init__(self, send_sems, recv_sems):
        self.send_sems, self.recv_sems = send_sems, recv_sems
        self.number = {}
        self.sent = []

    def copy(self, key, ref, device):
        number = self.number.setdefault(key, len(self.number))
        return pltpu.make_async_remote_copy(
            src_ref=ref[0],
            dst_ref=ref[1],
            send_sem=self.send_sems.at[number],
            recv_sem=self.recv_sems.at[number],
            device_id=device,
            device_id_type=MESH,
        )

    def send(self, key, src, dst, **steps):
        device = {axis: shifted(axis, step) for axis, step in steps.items()}
        copy = self.copy(key, (src, dst), device)
        copy.start()
        self.sent.append((key, copy))

    def wait(self, key, slot, axis):
        self.copy(key, (slot, slot), {axis: shifted(axis, 1)}).wait_recv()

    def flush(self, name=None):
        rest = []
        for key, copy in self.sent:
            if name in (None, key[0]):
                copy.wait_send()
            else:
                rest.append((key, copy))
        self.sent = rest


def gather_balanced(mail, name, slot, line, pair):
    def send(key, dl, dp, h, **steps):
        ref = slot(dl, dp, h)
        mail.send((name, *key, h), ref, ref, **steps)

    def wait(key, dl, dp, h, axis):
        mail.wait((name, *key, h), slot(dl, dp, h), axis)

    ways = (1, -1)
    for h in (0, 1):
        for way in ways:
            send(("l", way, 1, 0), 0, 0, h, **{line: way})
        send(("p", 0, 0), 0, 0, h, **{pair: 1})
    yield
    for h in (0, 1):
        for way in ways:
            wait(("l", way, 1, 0), -way, 0, h, line)
            send(("l", way, 2, 0), -way, 0, h, **{line: way})
            send(("p", way, 1), -way, 0, h, **{pair: 1})
    yield
    for h in (0, 1):
        for way in ways:
            wait(("l", way, 2, 0), -2 * way, 0, h, line)
            send(("l", way, 3, 0), -2 * way, 0, h, **{line: way})
            send(("p", way, 2), -2 * way, 0, h, **{pair: 1})
    for h in (0, 1):
        wait(("p", 0, 0), 0, 1, h, pair)
    yield
    for h in (0, 1):
        for way in ways:
            wait(("l", way, 3, 0), -3 * way, 0, h, line)
            if way == 1 - 2 * h:
                send(("l", way, 4, 0), -3 * way, 0, h, **{line: way})
        for way in ways:
            wait(("p", way, 2), -2 * way, 1, h, pair)
            send(("l", way, 3, 1), -2 * way, 1, h, **{line: way})
    for h in (0, 1):
        for way in ways:
            wait(("p", way, 1), -way, 1, h, pair)
    yield
    for h in (0, 1):
        way = 1 - 2 * h
        wait(("l", way, 3, 1), -3 * way, 1, h, line)
        send(("l", way, 4, 1), -3 * way, 1, h, **{line: way})
    yield
    for h in (0, 1):
        way = 2 * h - 1
        wait(("l", way, 3, 1), -3 * way, 1, h, line)
    for dp in (0, 1):
        for h in (0, 1):
            way = 1 - 2 * h
            wait(("l", way, 4, dp), -4 * way, dp, h, line)
    yield


ORDER = (
    (0, 0),
    (-1, 0),
    (1, 0),
    (-2, 0),
    (2, 0),
    (0, 1),
    (-3, 0),
    (3, 0),
    (-2, 1),
    (2, 1),
    (-1, 1),
    (1, 1),
    (-3, 1),
    (3, 1),
    (4, 0),
    (4, 1),
)
READY = (None, (0, 3), (3, 6), (6, 9), (9, 12), (12, 16))


def picked(place, first, last, values):
    found = jnp.int32(values[first])
    for number in range(first + 1, last):
        found = jnp.where(place == number, jnp.int32(values[number]), found)
    return found


def gather_ring(mail, name, slot, line):
    def send(way, d, h):
        ref = slot(way * (1 - d), h)
        mail.send((name, way, d, h), ref, ref, **{line: way})

    ways = (1, -1)
    for h in (0, 1):
        for way in ways:
            send(way, 1, h)
    yield
    for d in (1, 2, 3):
        for h in (0, 1):
            for way in ways:
                mail.wait((name, way, d, h), slot(-d * way, h), line)
                if d < 3 or way == 1 - 2 * h:
                    send(way, d + 1, h)
        yield
    for h in (0, 1):
        mail.wait((name, 1 - 2 * h, 4, h), slot(4, h), line)
    yield


RING_ORDER = (0, -1, 1, -2, 2, -3, 3, 4)
RING_READY = (None, (0, 3), (3, 5), (5, 7), (7, 8))


def scatter_balanced(
    mail, name, prepare, terms, outgoing, incoming, line, pair, early, result
):
    places, made = {}, {}
    half = result.shape[0] // 2

    def ready(*offsets):
        for dl, dp in offsets:
            at = made.setdefault((dl % 8, dp), len(made))
            terms[at] = prepare(dl, dp)

    def term(dl, dp, h):
        return terms[made[dl % 8, dp], pl.ds(h * half, half), :]

    def place(key):
        return places.setdefault(key, len(places))

    def send(key, value, **steps):
        at = place(key)
        outgoing[at] = value.astype(BF16)
        mail.send((name, *key), outgoing.at[at], incoming.at[at], **steps)

    def take(key, axis):
        at = place(key)
        mail.wait((name, *key), incoming.at[at], axis)
        return incoming[at].astype(F32)

    def send_near():
        for h in (0, 1):
            for way in ways:
                send(("p", way, 1, h), term(way, 1, h), **{pair: 1})
        for h in (0, 1):
            send(("p", 0, 0, h), term(0, 1, h), **{pair: 1})

    ways = (1, -1)
    ready((4, 0), (4, 1))
    for h in (0, 1):
        way = 1 - 2 * h
        for dp in (1, 0):
            send(("l", way, 4, dp, h), term(4, dp, h), **{line: way})
    yield
    ready((3, 1), (3, 0), (-3, 1), (-3, 0))
    for h in (0, 1):
        way = 2 * h - 1
        for dp in (1, 0):
            send(("l", way, 3, dp, h), term(3 * way, dp, h), **{line: way})
    if early:
        ready((1, 1), (-1, 1), (0, 1))
        send_near()
    for h in (0, 1):
        way = 1 - 2 * h
        for dp in (1, 0):
            total = term(3 * way, dp, h) + take(("l", way, 4, dp, h), line)
            send(("l", way, 3, dp, h), total, **{line: way})
    yield
    ready((2, 1), (-2, 1), (2, 0), (-2, 0))
    for h in (0, 1):
        for way in (2 * h - 1, 1 - 2 * h):
            total = term(2 * way, 1, h) + take(("l", way, 3, 1, h), line)
            send(("p", way, 2, h), total, **{pair: 1})
    yield
    if not early:
        ready((1, 1), (-1, 1), (0, 1))
        send_near()
    ready((1, 0), (-1, 0), (0, 0))
    for h in (0, 1):
        for way in (2 * h - 1, 1 - 2 * h):
            total = term(2 * way, 0, h) + take(("l", way, 3, 0, h), line)
            total = total + take(("p", way, 2, h), pair)
            send(("l", way, 2, h), total, **{line: way})
    yield
    for h in (0, 1):
        for way in ways:
            total = term(way, 0, h) + take(("p", way, 1, h), pair)
            total = total + take(("l", way, 2, h), line)
            send(("l", way, 1, h), total, **{line: way})
    yield
    for h in (0, 1):
        total = term(0, 0, h) + take(("p", 0, 0, h), pair)
        for way in ways:
            total = total + take(("l", way, 1, h), line)
        result[pl.ds(h * half, half), :] = total
    yield


def gather_line(mail, name, slot, line, pair, arrived):
    def send(key, dl, dp, **steps):
        ref = slot(dl, dp)
        mail.send((name, *key), ref, ref, **steps)

    def wait(key, dl, dp, axis):
        mail.wait((name, *key), slot(dl, dp), axis)

    ways = (1, -1)
    send(("p",), 0, 0, **{pair: 1})
    for way in ways:
        send(("l", way, 1, 0), 0, 0, **{line: way})
    arrived(0, 0)
    yield
    wait(("p",), 0, 1, pair)
    for way in ways:
        send(("l", way, 1, 1), 0, 1, **{line: way})
    arrived(0, 1)
    for d in (1, 2, 3):
        yield
        for dp in (0, 1):
            for way in ways:
                wait(("l", way, d, dp), -d * way, dp, line)
                if d < 3 or way == 1 - 2 * dp:
                    send(("l", way, d + 1, dp), -d * way, dp, **{line: way})
                arrived(-d * way, dp)
    yield
    for dp in (0, 1):
        wait(("l", 1 - 2 * dp, 4, dp), 4, dp, line)
        arrived(4, dp)
    yield


def packed_sum(grad, weight):
    size = jnp.abs(grad)
    spread = jnp.sqrt(jnp.mean(grad * grad, axis=-1, keepdims=True) + 1e-05)
    top = jnp.max(size, axis=-1, keepdims=True)
    largest = top / (top + spread) + 1e-06
    divisor = (size + spread) * largest
    inverse = pl.reciprocal(divisor, approx=True)
    inverse = inverse * (2.0 - divisor * inverse)
    quant = (grad * inverse).astype(BF16)
    return quant.astype(F32) * (weight * largest)


def kernel(
    x_hbm,
    t_hbm,
    wu_hbm,
    wd_hbm,
    mu_hbm,
    member_up,
    member_down,
    path_rate,
    mean_up,
    mean_down,
    x_ref,
    t_ref,
    wu_ref,
    mu_ref,
    turned,
    own_rows,
    down_all,
    x_out,
    x_in,
    d_out,
    d_in,
    dpre_all,
    hid_all,
    dh_ref,
    pre_ref,
    terms,
    first_out,
    first_in,
    second_out,
    second_in,
    acc_up,
    acc_down,
    sums_in,
    pair_out,
    pair_in,
    send_sems,
    recv_sems,
    local_sems,
):
    rows, width = x_ref.shape
    own_up, hidden = wu_ref.shape
    own_down = mean_down.shape[0]
    inv_width = width ** (-0.5)
    inv_hidden = hidden ** (-0.5)
    step = 512
    steps = width // step
    y, xl = lax.axis_index("y"), lax.axis_index("xl")
    xh, z, core = lax.axis_index("xh"), lax.axis_index("z"), lax.axis_index("core")
    row = y * 2 + xl
    col = xh * 16 + z * 2 + core
    chip = xh * 8 + z

    peers = [(dl, dp) for dl in (4, 3, -3, 2, -2, 1, -1, 0) for dp in (1, 0) if dl or dp]
    ring = (4, 3, -3, 2, -2, 1, -1)
    barrier = pltpu.get_barrier_semaphore()
    partners = [{"y": dl, "xl": dp} for dl, dp in peers]
    partners += [{"z": dl} for dl in ring] + [{"xh": 1}, {"core": 1}]
    for steps_to in partners:
        pl.semaphore_signal(
            barrier,
            inc=1,
            device_id={axis: shifted(axis, by) for axis, by in steps_to.items()},
            device_id_type=MESH,
        )

    def row_of(dl, dp):
        return lax.rem(y + (dl + 8), 8) * 2 + lax.rem(xl + dp, 2)

    def chip_of(dl, dp):
        return lax.rem(xh + dp, 2) * 8 + lax.rem(z + (dl + 8), 8)

    def col_of(dl, dp, dc):
        return chip_of(dl, dp) * 2 + lax.rem(core + dc, 2)

    def span(number, size):
        return pl.ds(pl.multiple_of(number * size, 16), size)

    def cut(ref, number, size):
        return ref.at[span(number, size)]

    mail = Mail(send_sems, recv_sems)
    half_hid = hidden // 2

    loads = [
        pltpu.make_async_copy(src, dst, local_sems.at[number])
        for number, (src, dst) in enumerate(
            (
                (x_hbm, x_ref),
                (wd_hbm, cut(down_all, col, own_down)),
                (wu_hbm, wu_ref),
                (t_hbm, t_ref),
                (mu_hbm, mu_ref),
            )
        )
    ]
    for load in loads:
        load.start()

    def down_slot(dl, dp, dc=0):
        return cut(down_all, col_of(dl, dp, dc), own_down)

    def dpre_slot(dl, dp, h):
        return dpre_all.at[row_of(dl, dp), pl.ds(h * half_hid, half_hid)]

    def z_of(dl):
        return lax.rem(z + (dl + 8), 8)

    def hid_slot(dl, h):
        return hid_all.at[z_of(dl), pl.ds(h * half_hid, half_hid)]

    def down_arrived(dl, dp):
        ref = down_slot(dl, dp)
        mail.send(("down sibling", dl % 8, dp), ref, ref, core=1)

    def send_delta(distances):
        for dl in ring:
            for v in (0, 1):
                if abs(dl) in distances:
                    mail.send(
                        ("delta", dl % 8, v),
                        cut(d_out, v * 8 + z_of(dl), 2 * own_down),
                        cut(d_in, z * 2 + v, 2 * own_down),
                        z=dl,
                    )

    def send_tokens(distances):
        for dl, dp in peers:
            if abs(dl) in distances:
                mail.send(
                    ("tokens", dl % 8, dp),
                    cut(x_out, row_of(dl, dp), own_up),
                    cut(x_in, row, own_up),
                    y=dl,
                    xl=dp,
                )

    loads[0].wait()

    def turn(j, carry):
        at = pl.multiple_of(j * 128, 128)
        x_out[pl.ds(at, 128), :] = x_ref[:, pl.ds(at, 128)].astype(F32).T.astype(BF16)
        return carry

    lax.fori_loop(0, width // 128, turn, 0, unroll=7)
    loads[1].wait()
    pl.semaphore_wait(barrier, len(partners))
    send_tokens((4,))
    down_steps = gather_line(mail, "down", down_slot, "z", "xh", down_arrived)

    x_in[span(row, own_up), :] = x_out[span(row, own_up), :]
    loads[2].wait()
    turned[...] = wu_ref[...].astype(F32).T.astype(BF16)
    mail.flush("tokens")
    send_tokens((3,))
    next(down_steps)
    loads[3].wait()

    def turn_delta(j, carry):
        at = pl.multiple_of(j * 128, 128)
        other = t_ref[:, pl.ds(at, 128)].astype(F32)
        d_out[pl.ds(at, 128), :] = (x_ref[:, pl.ds(at, 128)].astype(F32) - other).T.astype(BF16)
        return carry

    lax.fori_loop(0, width // 128, turn_delta, 0, unroll=7)

    here = {(0, 0)}

    def term(dl, dp):
        at = (dl % 8, dp)
        if at not in here:
            here.add(at)
            mail.wait(("tokens", -dl % 8, dp), cut(x_in, row_of(dl, dp), own_up), "y")
        return jnp.dot(
            turned[...], x_in[span(row_of(dl, dp), own_up), :], preferred_element_type=F32
        )

    first = scatter_balanced(
        mail, "first", term, terms, first_out, first_in, "y", "xl", False, pre_ref
    )
    next(first)
    next(down_steps)
    mail.flush("tokens")
    send_tokens((2,))
    next(first)
    next(down_steps)
    send_tokens((1, 0))
    next(first)
    next(down_steps)
    next(first)
    next(down_steps)
    next(first)
    next(down_steps)
    send_delta((4, 3))
    next(first)
    send_delta((2, 1))
    for dl in range(8):
        for dp in range(2):
            mail.wait(("down sibling", dl, dp), down_slot(dl, dp, 1), "core")
    for v in (0, 1):
        d_in[span(z * 2 + v, 2 * own_down), :] = d_out[span(v * 8 + z, 2 * own_down), :]
        own_rows[span(v, 2 * own_down), :] = down_all[span(v * 8 + z, 2 * own_down), :]

    pre = pre_ref[...].T * inv_width
    sig = jax.nn.sigmoid(pre)
    hid = (pre * sig).astype(BF16)
    slope = sig * (1.0 + pre * (1.0 - sig))

    dh_ref[...] = jnp.zeros_like(dh_ref)

    def back(k, carry):
        at = pl.multiple_of(k * step, step)
        piece = down_all[pl.ds(at, step), :]
        mixed = lax.dot_general(hid, piece, NT, preferred_element_type=F32) * inv_hidden
        dy = (
            x_ref[:, pl.ds(at, step)].astype(F32) + mixed - t_ref[:, pl.ds(at, step)].astype(F32)
        ).astype(BF16)
        dh_ref[...] += jnp.dot(dy, piece, preferred_element_type=F32)
        return carry

    lax.fori_loop(0, steps, back, 0, unroll=True)
    dpre = dh_ref[...] * inv_hidden * slope
    dpre_all[row] = dpre.T.astype(BF16)

    def ordered(number, between):
        dl = picked(number, *between, [dl for dl, _ in ORDER])
        dp = picked(number, *between, [dp for _, dp in ORDER])
        return dl, dp

    acc_up[...] = jnp.zeros_like(acc_up)

    def up_path(between, number, carry):
        p = row_of(*ordered(number, between))
        grad = (
            lax.dot_general(
                x_in[span(p, own_up), :], dpre_all[p], NT, preferred_element_type=F32
            )
            * inv_width
        )
        acc_up[...] += packed_sum(grad, member_up[p, col].astype(F32) * path_rate[p, col])
        return carry

    for between, _ in zip(READY, gather_balanced(mail, "dpre", dpre_slot, "y", "xl")):
        if between:
            lax.fori_loop(*between, functools.partial(up_path, between), 0, unroll=True)
    count_up = lax.fori_loop(
        0, N_ROW, lambda p, count: count + member_up[p, col].astype(F32), jnp.float32(0.0)
    )
    loads[4].wait()
    average = acc_up[...] / count_up
    mean_up[...] = average
    momentum = 0.9 * mu_ref[...] + average
    fresh = wu_ref[...].astype(F32) - 0.7 * (average + 0.9 * momentum)
    turned[...] = fresh.T.astype(BF16)

    for _ in scatter_balanced(
        mail, "second", term, terms, second_out, second_in, "y", "xl", True, pre_ref
    ):
        pass
    pre_again = pre_ref[...] * inv_width
    hid_all[z] = (pre_again * jax.nn.sigmoid(pre_again)).astype(BF16)

    acc_down[...] = jnp.zeros_like(acc_down)

    def down_path(between, number, carry):
        q = z_of(picked(number, *between, RING_ORDER))
        acts = hid_all[q]
        mixed = jnp.dot(own_rows[...], acts, preferred_element_type=F32) * inv_hidden
        dy = (d_in[span(q, 4 * own_down), :].astype(F32) + mixed).astype(BF16)
        grad = lax.dot_general(dy, acts, NT, preferred_element_type=F32) * inv_hidden
        c = xh * 16 + q * 2 + core
        weight = member_down[row, c].astype(F32) * path_rate[row, c]
        acc_down[...] += packed_sum(grad, weight)
        return carry

    for between, _ in zip(RING_READY, gather_ring(mail, "hid", hid_slot, "z")):
        if between:
            first_place, last_place = between
            for dl in RING_ORDER[first_place:last_place]:
                for v in (0, 1):
                    if dl:
                        mail.wait(
                            ("delta", -dl % 8, v), cut(d_in, z_of(dl) * 2 + v, 2 * own_down), "z"
                        )
            lax.fori_loop(*between, functools.partial(down_path, between), 0, unroll=True)
    for v in (0, 1):
        mail.send(
            ("sums", v),
            cut(acc_down, v * 2 + 1 - core, own_down),
            cut(sums_in, v, own_down),
            core=1,
        )
    count_down = lax.fori_loop(
        0, N_COL, lambda q, count: count + member_down[row, q].astype(F32), jnp.float32(0.0)
    )
    for v in (0, 1):
        mail.wait(("sums", v), cut(sums_in, v, own_down), "core")

    def both_cores(v):
        return acc_down[span(v * 2 + core, own_down), :] + sums_in[span(v, own_down), :]

    pair_out[...] = both_cores(1 - xh).astype(BF16)
    mail.send(("pair",), pair_out, pair_in, xh=1)
    own_sums = both_cores(xh)
    mail.wait(("pair",), pair_in, "xh")
    mean_down[...] = (own_sums + pair_in[...].astype(F32)) / count_down
    mail.flush()


def per_device(
    tokens, targets, w_up, w_down, up_momentum, down_momentum, member_up, member_down, path_rate
):
    rows, width = tokens.shape
    own_up, hidden = w_up.shape[1:]
    own_down = w_down.shape[1]
    vmem = pl.BlockSpec(memory_space=pltpu.VMEM)
    smem = pl.BlockSpec(memory_space=pltpu.SMEM)
    messages, sums = 200, 30
    means = pl.pallas_call(
        kernel,
        out_shape=(
            jax.ShapeDtypeStruct((own_up, hidden), F32),
            jax.ShapeDtypeStruct((own_down, hidden), F32),
        ),
        in_specs=[pl.BlockSpec(memory_space=pl.ANY)] * 5 + [smem] * 3,
        out_specs=(vmem,) * 2,
        scratch_shapes=[
            pltpu.VMEM((rows, width), BF16),
            pltpu.VMEM((rows, width), BF16),
            pltpu.VMEM((own_up, hidden), BF16),
            pltpu.VMEM((own_up, hidden), F32),
            pltpu.VMEM((hidden, own_up), BF16),
            pltpu.VMEM((4 * own_down, hidden), BF16),
            pltpu.VMEM((width, hidden), BF16),
            pltpu.VMEM((width, rows), BF16),
            pltpu.VMEM((width, rows), BF16),
            pltpu.VMEM((width, rows), BF16),
            pltpu.VMEM((width, rows), BF16),
            pltpu.VMEM((N_ROW, hidden, rows), BF16),
            pltpu.VMEM((AXES["z"], hidden, rows), BF16),
            pltpu.VMEM((rows, hidden), F32),
            pltpu.VMEM((hidden, rows), F32),
            pltpu.VMEM((N_ROW, hidden, rows), F32),
            pltpu.VMEM((sums, hidden // 2, rows), BF16),
            pltpu.VMEM((sums, hidden // 2, rows), BF16),
            pltpu.VMEM((sums, hidden // 2, rows), BF16),
            pltpu.VMEM((sums, hidden // 2, rows), BF16),
            pltpu.VMEM((own_up, hidden), F32),
            pltpu.VMEM((4 * own_down, hidden), F32),
            pltpu.VMEM((2 * own_down, hidden), F32),
            pltpu.VMEM((own_down, hidden), BF16),
            pltpu.VMEM((own_down, hidden), BF16),
            pltpu.SemaphoreType.DMA((messages,)),
            pltpu.SemaphoreType.DMA((messages,)),
            pltpu.SemaphoreType.DMA((5,)),
        ],
        compiler_params=pltpu.CompilerParams(
            collective_id=0, has_side_effects=True, vmem_limit_bytes=56 * 1024 * 1024
        ),
        name="path_mixture",
    )(
        tokens,
        targets,
        w_up[0],
        w_down[0],
        up_momentum[0],
        member_up,
        member_down,
        path_rate,
    )
    outs = []
    for matrix, old, mean in ((w_up, up_momentum, means[0]), (w_down, down_momentum, means[1])):
        momentum = 0.9 * old + mean[None]
        fresh = matrix.astype(F32) - 0.7 * (mean[None] + 0.9 * momentum)
        outs += [fresh.astype(BF16), momentum]
    return tuple(outs)


def solution(mesh):
    torus = Mesh(mesh.devices.reshape(tuple(AXES.values())), tuple(AXES))
    placed = (
        P(ROW + COL, None),
        P(ROW + COL, None),
        P(COL, ROW, None),
        P(ROW, COL, None),
        P(COL, ROW, None),
        P(ROW, COL, None),
        P(),
        P(),
        P(),
    )
    return jax.shard_map(
        per_device,
        mesh=torus,
        in_specs=placed,
        out_specs=(
            P(COL, ROW, None),
            P(COL, ROW, None),
            P(ROW, COL, None),
            P(ROW, COL, None),
        ),
        check_vma=False,
    )
```

```python
import functools

import jax
import jax.numpy as jnp
from jax import lax
from jax.experimental import pallas as pl
from jax.experimental.pallas import tpu as pltpu
from jax.sharding import Mesh
from jax.sharding import PartitionSpec as P

MESH = pl.DeviceIdType.MESH
F32 = jnp.float32
BF16 = jnp.bfloat16
AXES = {"y": 8, "xl": 2, "xh": 2, "z": 8, "core": 2}
ROW = ("y", "xl")
COL = ("xh", "z", "core")
N_ROW, N_COL = 16, 32
NT = (((1,), (1,)), ((), ()))


def shifted(axis, step):
    size = AXES[axis]
    return lax.rem(lax.axis_index(axis) + (step % size), size)


class Mail:
    def __init__(self, send_sems, recv_sems):
        self.send_sems, self.recv_sems = send_sems, recv_sems
        self.number = {}
        self.sent = []

    def copy(self, key, ref, device):
        number = self.number.setdefault(key, len(self.number))
        return pltpu.make_async_remote_copy(
            src_ref=ref[0],
            dst_ref=ref[1],
            send_sem=self.send_sems.at[number],
            recv_sem=self.recv_sems.at[number],
            device_id=device,
            device_id_type=MESH,
        )

    def send(self, key, src, dst, **steps):
        device = {axis: shifted(axis, step) for axis, step in steps.items()}
        copy = self.copy(key, (src, dst), device)
        copy.start()
        self.sent.append((key, copy))

    def wait(self, key, slot, axis):
        self.copy(key, (slot, slot), {axis: shifted(axis, 1)}).wait_recv()

    def flush(self, name=None):
        rest = []
        for key, copy in self.sent:
            if name in (None, key[0]):
                copy.wait_send()
            else:
                rest.append((key, copy))
        self.sent = rest


def gather_balanced(mail, name, slot, line, pair):
    def send(key, dl, dp, h, **steps):
        ref = slot(dl, dp, h)
        mail.send((name, *key, h), ref, ref, **steps)

    def wait(key, dl, dp, h, axis):
        mail.wait((name, *key, h), slot(dl, dp, h), axis)

    ways = (1, -1)
    for h in (0, 1):
        for way in ways:
            send(("l", way, 1, 0), 0, 0, h, **{line: way})
        send(("p", 0, 0), 0, 0, h, **{pair: 1})
    yield
    for h in (0, 1):
        for way in ways:
            wait(("l", way, 1, 0), -way, 0, h, line)
            send(("l", way, 2, 0), -way, 0, h, **{line: way})
            send(("p", way, 1), -way, 0, h, **{pair: 1})
    yield
    for h in (0, 1):
        for way in ways:
            wait(("l", way, 2, 0), -2 * way, 0, h, line)
            send(("l", way, 3, 0), -2 * way, 0, h, **{line: way})
            send(("p", way, 2), -2 * way, 0, h, **{pair: 1})
    for h in (0, 1):
        wait(("p", 0, 0), 0, 1, h, pair)
    yield
    for h in (0, 1):
        for way in ways:
            wait(("l", way, 3, 0), -3 * way, 0, h, line)
            if way == 1 - 2 * h:
                send(("l", way, 4, 0), -3 * way, 0, h, **{line: way})
        for way in ways:
            wait(("p", way, 2), -2 * way, 1, h, pair)
            send(("l", way, 3, 1), -2 * way, 1, h, **{line: way})
    for h in (0, 1):
        for way in ways:
            wait(("p", way, 1), -way, 1, h, pair)
    yield
    for h in (0, 1):
        way = 1 - 2 * h
        wait(("l", way, 3, 1), -3 * way, 1, h, line)
        send(("l", way, 4, 1), -3 * way, 1, h, **{line: way})
    yield
    for h in (0, 1):
        way = 2 * h - 1
        wait(("l", way, 3, 1), -3 * way, 1, h, line)
    for dp in (0, 1):
        for h in (0, 1):
            way = 1 - 2 * h
            wait(("l", way, 4, dp), -4 * way, dp, h, line)
    yield


ORDER = (
    (0, 0),
    (-1, 0),
    (1, 0),
    (-2, 0),
    (2, 0),
    (0, 1),
    (-3, 0),
    (3, 0),
    (-2, 1),
    (2, 1),
    (-1, 1),
    (1, 1),
    (-3, 1),
    (3, 1),
    (4, 0),
    (4, 1),
)
READY = (None, (0, 3), (3, 6), (6, 9), (9, 12), (12, 16))


def picked(place, first, last, values):
    found = jnp.int32(values[first])
    for number in range(first + 1, last):
        found = jnp.where(place == number, jnp.int32(values[number]), found)
    return found


def gather_ring(mail, name, slot, line, pieces):
    def send(way, d, h):
        ref = slot(way * (1 - d), h)
        mail.send((name, way, d, h), ref, ref, **{line: way})

    ways = (1, -1)
    last_way = [1 if 2 * h < pieces else -1 for h in range(pieces)]
    for h in range(pieces):
        for way in ways:
            send(way, 1, h)
        if 2 * (h + 1) in (pieces, 2 * pieces):
            yield
    for d in (1, 2, 3):
        for h in range(pieces):
            for way in ways:
                mail.wait((name, way, d, h), slot(-d * way, h), line)
                if d < 3 or way == last_way[h]:
                    send(way, d + 1, h)
        yield
    for h in range(pieces):
        mail.wait((name, last_way[h], 4, h), slot(4, h), line)
    yield


RING_ORDER = (0, -1, 1, -2, 2, -3, 3, 4)
RING_READY = ((0, 3), (3, 5), (5, 7), (7, 8))


def scatter_balanced(
    mail, name, prepare, terms, outgoing, incoming, line, pair, early, result
):
    places, made = {}, {}
    half = result.shape[0] // 2

    def ready(*offsets):
        for dl, dp in offsets:
            at = made.setdefault((dl % 8, dp), len(made))
            terms[at] = prepare(dl, dp)

    def term(dl, dp, h):
        return terms[made[dl % 8, dp], pl.ds(h * half, half), :]

    def place(key):
        return places.setdefault(key, len(places))

    def send(key, value, **steps):
        at = place(key)
        outgoing[at] = value.astype(BF16)
        mail.send((name, *key), outgoing.at[at], incoming.at[at], **steps)

    def take(key, axis):
        at = place(key)
        mail.wait((name, *key), incoming.at[at], axis)
        return incoming[at].astype(F32)

    def send_near():
        for h in (0, 1):
            for way in ways:
                send(("p", way, 1, h), term(way, 1, h), **{pair: 1})
        for h in (0, 1):
            send(("p", 0, 0, h), term(0, 1, h), **{pair: 1})

    ways = (1, -1)
    ready((4, 0), (4, 1))
    for h in (0, 1):
        way = 1 - 2 * h
        for dp in (1, 0):
            send(("l", way, 4, dp, h), term(4, dp, h), **{line: way})
    yield
    ready((3, 1), (3, 0), (-3, 1), (-3, 0))
    for h in (0, 1):
        way = 2 * h - 1
        for dp in (1, 0):
            send(("l", way, 3, dp, h), term(3 * way, dp, h), **{line: way})
    if early:
        ready((1, 1), (-1, 1), (0, 1))
        send_near()
    for h in (0, 1):
        way = 1 - 2 * h
        for dp in (1, 0):
            total = term(3 * way, dp, h) + take(("l", way, 4, dp, h), line)
            send(("l", way, 3, dp, h), total, **{line: way})
    yield
    ready((2, 1), (-2, 1), (2, 0), (-2, 0))
    for h in (0, 1):
        for way in (2 * h - 1, 1 - 2 * h):
            total = term(2 * way, 1, h) + take(("l", way, 3, 1, h), line)
            send(("p", way, 2, h), total, **{pair: 1})
    yield
    if not early:
        ready((1, 1), (-1, 1), (0, 1))
        send_near()
    ready((1, 0), (-1, 0), (0, 0))
    for h in (0, 1):
        for way in (2 * h - 1, 1 - 2 * h):
            total = term(2 * way, 0, h) + take(("l", way, 3, 0, h), line)
            total = total + take(("p", way, 2, h), pair)
            send(("l", way, 2, h), total, **{line: way})
    yield
    for h in (0, 1):
        for way in ways:
            total = term(way, 0, h) + take(("p", way, 1, h), pair)
            total = total + take(("l", way, 2, h), line)
            send(("l", way, 1, h), total, **{line: way})
    yield
    for h in (0, 1):
        total = term(0, 0, h) + take(("p", 0, 0, h), pair)
        for way in ways:
            total = total + take(("l", way, 1, h), line)
        result[pl.ds(h * half, half), :] = total
        yield


def gather_line(mail, name, slot, line, pair, arrived):
    def send(key, dl, dp, **steps):
        ref = slot(dl, dp)
        mail.send((name, *key), ref, ref, **steps)

    def wait(key, dl, dp, axis):
        mail.wait((name, *key), slot(dl, dp), axis)

    ways = (1, -1)
    send(("p",), 0, 0, **{pair: 1})
    for way in ways:
        send(("l", way, 1, 0), 0, 0, **{line: way})
    arrived(0, 0)
    yield
    wait(("p",), 0, 1, pair)
    for way in ways:
        send(("l", way, 1, 1), 0, 1, **{line: way})
    arrived(0, 1)
    for d in (1, 2, 3):
        yield
        for dp in (0, 1):
            for way in ways:
                wait(("l", way, d, dp), -d * way, dp, line)
                if d < 3 or way == 1 - 2 * dp:
                    send(("l", way, d + 1, dp), -d * way, dp, **{line: way})
                arrived(-d * way, dp)
    yield
    for dp in (0, 1):
        wait(("l", 1 - 2 * dp, 4, dp), 4, dp, line)
        arrived(4, dp)
    yield


def packed_sum(grad, weight):
    size = jnp.abs(grad)
    spread = jnp.sqrt(jnp.mean(grad * grad, axis=-1, keepdims=True) + 1e-05)
    top = jnp.max(size, axis=-1, keepdims=True)
    largest = top / (top + spread) + 1e-06
    divisor = (size + spread) * largest
    inverse = pl.reciprocal(divisor, approx=True)
    inverse = inverse * (2.0 - divisor * inverse)
    quant = (grad * inverse).astype(BF16)
    return quant.astype(F32) * (weight * largest)


def kernel(
    x_hbm,
    t_hbm,
    wu_hbm,
    wd_hbm,
    mu_hbm,
    member_up,
    member_down,
    path_rate,
    mean_up,
    mean_down,
    x_ref,
    t_ref,
    wu_ref,
    mu_ref,
    turned,
    own_rows,
    down_all,
    x_out,
    x_in,
    d_out,
    d_in,
    dpre_all,
    hid_all,
    dh_ref,
    pre_ref,
    terms,
    first_out,
    first_in,
    second_out,
    second_in,
    acc_up,
    acc_down,
    sums_in,
    pair_out,
    pair_in,
    send_sems,
    recv_sems,
    local_sems,
):
    rows, width = x_ref.shape
    own_up, hidden = wu_ref.shape
    own_down = mean_down.shape[0]
    inv_width = width ** (-0.5)
    inv_hidden = hidden ** (-0.5)
    step = 512
    steps = width // step
    y, xl = lax.axis_index("y"), lax.axis_index("xl")
    xh, z, core = lax.axis_index("xh"), lax.axis_index("z"), lax.axis_index("core")
    row = y * 2 + xl
    col = xh * 16 + z * 2 + core
    chip = xh * 8 + z

    peers = [(dl, dp) for dl in (4, 3, -3, 2, -2, 1, -1, 0) for dp in (1, 0) if dl or dp]
    ring = (4, 3, -3, 2, -2, 1, -1)
    barrier = pltpu.get_barrier_semaphore()
    partners = [{"y": dl, "xl": dp} for dl, dp in peers]
    partners += [{"z": dl} for dl in ring] + [{"xh": 1}, {"core": 1}]
    for steps_to in partners:
        pl.semaphore_signal(
            barrier,
            inc=1,
            device_id={axis: shifted(axis, by) for axis, by in steps_to.items()},
            device_id_type=MESH,
        )

    def row_of(dl, dp):
        return lax.rem(y + (dl + 8), 8) * 2 + lax.rem(xl + dp, 2)

    def chip_of(dl, dp):
        return lax.rem(xh + dp, 2) * 8 + lax.rem(z + (dl + 8), 8)

    def col_of(dl, dp, dc):
        return chip_of(dl, dp) * 2 + lax.rem(core + dc, 2)

    def span(number, size):
        return pl.ds(pl.multiple_of(number * size, 16), size)

    def cut(ref, number, size):
        return ref.at[span(number, size)]

    mail = Mail(send_sems, recv_sems)
    half_hid = hidden // 2
    pieces = 2

    loads = [
        pltpu.make_async_copy(src, dst, local_sems.at[number])
        for number, (src, dst) in enumerate(
            (
                (x_hbm, x_ref),
                (wd_hbm, cut(down_all, col, own_down)),
                (wu_hbm, wu_ref),
                (t_hbm, t_ref),
                (mu_hbm, mu_ref),
            )
        )
    ]
    for load in loads:
        load.start()

    def down_slot(dl, dp, dc=0):
        return cut(down_all, col_of(dl, dp, dc), own_down)

    def dpre_slot(dl, dp, h):
        return dpre_all.at[row_of(dl, dp), pl.ds(h * half_hid, half_hid)]

    def z_of(dl):
        return lax.rem(z + (dl + 8), 8)

    def hid_slot(dl, h):
        size = hidden // pieces
        return hid_all.at[z_of(dl), pl.ds(h * size, size)]

    def down_arrived(dl, dp):
        ref = down_slot(dl, dp)
        mail.send(("down sibling", dl % 8, dp), ref, ref, core=1)

    def send_delta(distances):
        for dl in ring:
            for v in (0, 1):
                if abs(dl) in distances:
                    mail.send(
                        ("delta", dl % 8, v),
                        cut(d_out, v * 8 + z_of(dl), 2 * own_down),
                        cut(d_in, z * 2 + v, 2 * own_down),
                        z=dl,
                    )

    def send_tokens(distances):
        for dl, dp in peers:
            if abs(dl) in distances:
                mail.send(
                    ("tokens", dl % 8, dp),
                    cut(x_out, row_of(dl, dp), own_up),
                    cut(x_in, row, own_up),
                    y=dl,
                    xl=dp,
                )

    loads[0].wait()

    def turn(j, carry):
        at = pl.multiple_of(j * 128, 128)
        x_out[pl.ds(at, 128), :] = x_ref[:, pl.ds(at, 128)].astype(F32).T.astype(BF16)
        return carry

    lax.fori_loop(0, width // 128, turn, 0, unroll=7)
    loads[1].wait()
    pl.semaphore_wait(barrier, len(partners))
    send_tokens((4,))
    down_steps = gather_line(mail, "down", down_slot, "z", "xh", down_arrived)

    x_in[span(row, own_up), :] = x_out[span(row, own_up), :]
    loads[2].wait()
    turned[...] = wu_ref[...].astype(F32).T.astype(BF16)

    send_tokens((3,))
    next(down_steps)
    loads[3].wait()

    def turn_delta(j, carry):
        at = pl.multiple_of(j * 128, 128)
        other = t_ref[:, pl.ds(at, 128)].astype(F32)
        d_out[pl.ds(at, 128), :] = (x_ref[:, pl.ds(at, 128)].astype(F32) - other).T.astype(BF16)
        return carry

    lax.fori_loop(0, width // 128, turn_delta, 0, unroll=7)

    here = {(0, 0)}

    def term(dl, dp):
        at = (dl % 8, dp)
        if at not in here:
            here.add(at)
            mail.wait(("tokens", -dl % 8, dp), cut(x_in, row_of(dl, dp), own_up), "y")
        return jnp.dot(
            turned[...], x_in[span(row_of(dl, dp), own_up), :], preferred_element_type=F32
        )

    first = scatter_balanced(
        mail, "first", term, terms, first_out, first_in, "y", "xl", False, pre_ref
    )
    next(first)
    next(down_steps)

    send_tokens((2,))
    next(first)
    next(down_steps)
    send_tokens((1, 0))
    next(first)
    next(down_steps)
    next(first)
    next(down_steps)
    next(first)
    next(down_steps)
    next(first)
    next(first)
    for dl in range(8):
        for dp in range(2):
            mail.wait(("down sibling", dl, dp), down_slot(dl, dp, 1), "core")
    for v in (0, 1):
        d_in[span(z * 2 + v, 2 * own_down), :] = d_out[span(v * 8 + z, 2 * own_down), :]
        own_rows[span(v, 2 * own_down), :] = down_all[span(v * 8 + z, 2 * own_down), :]

    pre = pre_ref[...].T * inv_width
    sig = jax.nn.sigmoid(pre)
    hid = (pre * sig).astype(BF16)
    slope = sig * (1.0 + pre * (1.0 - sig))

    dh_ref[...] = jnp.zeros_like(dh_ref)

    def back(k, carry):
        at = pl.multiple_of(k * step, step)
        piece = down_all[pl.ds(at, step), :]
        mixed = lax.dot_general(hid, piece, NT, preferred_element_type=F32) * inv_hidden
        dy = (
            x_ref[:, pl.ds(at, step)].astype(F32) + mixed - t_ref[:, pl.ds(at, step)].astype(F32)
        ).astype(BF16)
        dh_ref[...] += jnp.dot(dy, piece, preferred_element_type=F32)
        return carry

    lax.fori_loop(0, steps, back, 0, unroll=True)
    dpre = dh_ref[...] * inv_hidden * slope
    dpre_all[row] = dpre.T.astype(BF16)

    def ordered(number, between):
        dl = picked(number, *between, [dl for dl, _ in ORDER])
        dp = picked(number, *between, [dp for _, dp in ORDER])
        return dl, dp

    acc_up[...] = jnp.zeros_like(acc_up)

    def up_path(between, number, carry):
        p = row_of(*ordered(number, between))
        grad = (
            lax.dot_general(
                x_in[span(p, own_up), :], dpre_all[p], NT, preferred_element_type=F32
            )
            * inv_width
        )
        acc_up[...] += packed_sum(grad, member_up[p, col].astype(F32) * path_rate[p, col])
        return carry

    for between, _ in zip(READY, gather_balanced(mail, "dpre", dpre_slot, "y", "xl")):
        if between:
            lax.fori_loop(*between, functools.partial(up_path, between), 0, unroll=True)
    send_delta((4, 3, 2, 1))
    count_up = lax.fori_loop(
        0, N_ROW, lambda p, count: count + member_up[p, col].astype(F32), jnp.float32(0.0)
    )
    loads[4].wait()
    average = acc_up[...] / count_up
    mean_up[...] = average
    momentum = 0.9 * mu_ref[...] + average
    fresh = wu_ref[...].astype(F32) - 0.7 * (average + 0.9 * momentum)
    turned[...] = fresh.T.astype(BF16)

    hid_steps = gather_ring(mail, "hid", hid_slot, "z", pieces)
    second = scatter_balanced(
        mail, "second", term, terms, second_out, second_in, "y", "xl", True, pre_ref
    )
    for stage, _ in enumerate(second):
        if stage >= 5:
            at = pl.ds((stage - 5) * half_hid, half_hid)
            pre_again = pre_ref[at, :] * inv_width
            hid_all[z, at, :] = (pre_again * jax.nn.sigmoid(pre_again)).astype(BF16)
            next(hid_steps)

    acc_down[...] = jnp.zeros_like(acc_down)

    def down_path(between, number, carry):
        q = z_of(picked(number, *between, RING_ORDER))
        acts = hid_all[q]
        mixed = jnp.dot(own_rows[...], acts, preferred_element_type=F32) * inv_hidden
        dy = (d_in[span(q, 4 * own_down), :].astype(F32) + mixed).astype(BF16)
        grad = lax.dot_general(dy, acts, NT, preferred_element_type=F32) * inv_hidden
        c = xh * 16 + q * 2 + core
        weight = member_down[row, c].astype(F32) * path_rate[row, c]
        acc_down[...] += packed_sum(grad, weight)
        return carry

    for between, _ in zip(RING_READY, hid_steps):
        if between:
            first_place, last_place = between
            for dl in RING_ORDER[first_place:last_place]:
                for v in (0, 1):
                    if dl:
                        mail.wait(
                            ("delta", -dl % 8, v), cut(d_in, z_of(dl) * 2 + v, 2 * own_down), "z"
                        )
            lax.fori_loop(*between, functools.partial(down_path, between), 0, unroll=True)
    for v in (0, 1):
        mail.send(
            ("sums", v),
            cut(acc_down, v * 2 + 1 - core, own_down),
            cut(sums_in, v, own_down),
            core=1,
        )
    count_down = lax.fori_loop(
        0, N_COL, lambda q, count: count + member_down[row, q].astype(F32), jnp.float32(0.0)
    )
    for v in (0, 1):
        mail.wait(("sums", v), cut(sums_in, v, own_down), "core")

    def both_cores(v):
        return acc_down[span(v * 2 + core, own_down), :] + sums_in[span(v, own_down), :]

    pair_out[...] = both_cores(1 - xh).astype(BF16)
    mail.send(("pair",), pair_out, pair_in, xh=1)
    own_sums = both_cores(xh)
    mail.wait(("pair",), pair_in, "xh")
    mean_down[...] = (own_sums + pair_in[...].astype(F32)) / count_down
    mail.flush()


def per_device(
    tokens, targets, w_up, w_down, up_momentum, down_momentum, member_up, member_down, path_rate
):
    rows, width = tokens.shape
    own_up, hidden = w_up.shape[1:]
    own_down = w_down.shape[1]
    vmem = pl.BlockSpec(memory_space=pltpu.VMEM)
    smem = pl.BlockSpec(memory_space=pltpu.SMEM)
    messages, sums = 240, 30
    means = pl.pallas_call(
        kernel,
        out_shape=(
            jax.ShapeDtypeStruct((own_up, hidden), F32),
            jax.ShapeDtypeStruct((own_down, hidden), F32),
        ),
        in_specs=[pl.BlockSpec(memory_space=pl.ANY)] * 5 + [smem] * 3,
        out_specs=(vmem,) * 2,
        scratch_shapes=[
            pltpu.VMEM((rows, width), BF16),
            pltpu.VMEM((rows, width), BF16),
            pltpu.VMEM((own_up, hidden), BF16),
            pltpu.VMEM((own_up, hidden), F32),
            pltpu.VMEM((hidden, own_up), BF16),
            pltpu.VMEM((4 * own_down, hidden), BF16),
            pltpu.VMEM((width, hidden), BF16),
            pltpu.VMEM((width, rows), BF16),
            pltpu.VMEM((width, rows), BF16),
            pltpu.VMEM((width, rows), BF16),
            pltpu.VMEM((width, rows), BF16),
            pltpu.VMEM((N_ROW, hidden, rows), BF16),
            pltpu.VMEM((AXES["z"], hidden, rows), BF16),
            pltpu.VMEM((rows, hidden), F32),
            pltpu.VMEM((hidden, rows), F32),
            pltpu.VMEM((N_ROW, hidden, rows), F32),
            pltpu.VMEM((sums, hidden // 2, rows), BF16),
            pltpu.VMEM((sums, hidden // 2, rows), BF16),
            pltpu.VMEM((sums, hidden // 2, rows), BF16),
            pltpu.VMEM((sums, hidden // 2, rows), BF16),
            pltpu.VMEM((own_up, hidden), F32),
            pltpu.VMEM((4 * own_down, hidden), F32),
            pltpu.VMEM((2 * own_down, hidden), F32),
            pltpu.VMEM((own_down, hidden), BF16),
            pltpu.VMEM((own_down, hidden), BF16),
            pltpu.SemaphoreType.DMA((messages,)),
            pltpu.SemaphoreType.DMA((messages,)),
            pltpu.SemaphoreType.DMA((5,)),
        ],
        compiler_params=pltpu.CompilerParams(
            collective_id=0, has_side_effects=True, vmem_limit_bytes=56 * 1024 * 1024
        ),
        name="path_mixture",
    )(
        tokens,
        targets,
        w_up[0],
        w_down[0],
        up_momentum[0],
        member_up,
        member_down,
        path_rate,
    )
    outs = []
    for matrix, old, mean in ((w_up, up_momentum, means[0]), (w_down, down_momentum, means[1])):
        momentum = 0.9 * old + mean[None]
        fresh = matrix.astype(F32) - 0.7 * (mean[None] + 0.9 * momentum)
        outs += [fresh.astype(BF16), momentum]
    return tuple(outs)


def solution(mesh):
    torus = Mesh(mesh.devices.reshape(tuple(AXES.values())), tuple(AXES))
    placed = (
        P(ROW + COL, None),
        P(ROW + COL, None),
        P(COL, ROW, None),
        P(ROW, COL, None),
        P(COL, ROW, None),
        P(ROW, COL, None),
        P(),
        P(),
        P(),
    )
    return jax.shard_map(
        per_device,
        mesh=torus,
        in_specs=placed,
        out_specs=(
            P(COL, ROW, None),
            P(COL, ROW, None),
            P(ROW, COL, None),
            P(ROW, COL, None),
        ),
        check_vma=False,
    )
```
